32 devices in a mesh: lm: 8 (over y, x, core), kf: 4 (over z).
Axes of the slice: x: 2, y: 2, z: 4, core: 2. Of those that a mesh axis runs over, the one named last changes fastest.
Arguments:
- land_rhs: float32 [3, 131072], P(None, ('lm', 'kf')), may hold values from -6 to 6
- key_rhs: float32 [15, 16384], P(None, ('lm', 'kf')), may hold values from -6 to 6
- land_damp: float32 [3, 131072], P(None, ('lm', 'kf')), may hold values from 0.5 to 2
- key_damp: float32 [15, 16384], P(None, ('lm', 'kf')), may hold values from 0.5 to 2
- land_jac: float32 [6, 524288], P(None, ('lm', 'kf')), may hold values from -4 to 4
- key_jac: float32 [30, 524288], P(None, ('lm', 'kf')), may hold values from -1.5 to 1.5
- obs_landmark: int32 [524288], P(('lm', 'kf')), may hold values from 0 to 16383, as said below
- obs_keyframe: int32 [524288], P(('lm', 'kf')), may hold values from 0 to 16383, as said below
- live_blocks: int32 [32], P(('lm', 'kf')), may hold values from 32 to 128, as said below
- preint: float32 [240, 245760], P(None, ('lm', 'kf')), as said below
Outputs:
- sol_land: float32 [3, 131072], P(None, ('lm', 'kf'))
- sol_key: float32 [15, 16384], P(None, ('lm', 'kf'))
The draws below stay inside these ranges and needn't reach their ends.
Inputs may be any that keep to these rules, and one draw needn't show every extreme that they name: `obs_landmark`: offsets among the 16384 landmarks of the lm index of the device holding the row. `obs_keyframe`: row o names a state s whose device index (s // 512) has the same kf index as the device holding row o. `live_blocks`: blocks past a device's count are padding; some device uses all its blocks. `preint`: each window's block is symmetric, and its diagonal exceeds the sum of magnitudes off the diagonal in its row.
All inputs are finite; a program needn't handle non-finite values.
Results may differ from the reference program's by a relative error of at most 0.0001.
Values sent between devices are 32-bit elements; how exact they have to be, the bound alone decides.
A program may use at most 128 MiB of HBM per device.

```python
import math
import jax
import jax.numpy as jnp
from jax import lax

WSTATES = 16
SDIM = 15
BLOCK = 128
OBLK = 128
ITERS = 2
LM_GROUPS = 8
KF_GROUPS = 4
LDEV = 4096
SDEV = 512
WPAR = 240
LANDMARKS = 131072
STATES = 16384
WINDOWS = 1024
OBS = 524288


def draw_obs_landmark(key, part):
    count = OBLK * BLOCK * LM_GROUPS * KF_GROUPS
    return jax.random.randint(jax.random.fold_in(key, 11), (count,), 0, KF_GROUPS * LDEV, dtype=jnp.int32)


def draw_obs_keyframe(key, part):
    count = OBLK * BLOCK * LM_GROUPS * KF_GROUPS
    row_ids = jnp.arange(count, dtype=jnp.int32)
    kf_col = row_ids // (OBLK * BLOCK) % KF_GROUPS
    first_key = jax.random.fold_in(key, 21)
    second_key = jax.random.fold_in(key, 22)
    lm_pick = jax.random.randint(first_key, (count,), 0, LM_GROUPS, dtype=jnp.int32)
    offset = jax.random.randint(second_key, (count,), 0, SDEV, dtype=jnp.int32)
    return (lm_pick * KF_GROUPS + kf_col) * SDEV + offset


def draw_live_blocks(key, part):
    first_key = jax.random.fold_in(key, 31)
    second_key = jax.random.fold_in(key, 32)
    devices = LM_GROUPS * KF_GROUPS
    lowest = max(1, OBLK // 4)
    counts = jax.random.randint(first_key, (devices,), lowest, OBLK + 1, dtype=jnp.int32)
    position = jax.random.randint(second_key, (), 0, devices, dtype=jnp.int32)
    return counts.at[position].set(OBLK)


def draw_preint(key, part):
    first_key = jax.random.fold_in(key, 41)
    second_key = jax.random.fold_in(key, 42)
    random_part = jax.random.uniform(first_key, (WINDOWS, WPAR, WPAR), jnp.float32, -1.0, 1.0) / (WPAR - 1)
    symmetric = 0.5 * (random_part + jnp.swapaxes(random_part, 1, 2))
    identity = jnp.eye(WPAR, dtype=jnp.float32)
    diagonal = jax.random.uniform(second_key, (WINDOWS, WPAR), jnp.float32, 1.1, 2.2)
    blocks = symmetric * (1.0 - identity) + identity * diagonal[:, :, None]
    return blocks.transpose(1, 0, 2).reshape(WPAR, WINDOWS * WPAR)


def levels(rng, shape, pieces, least, high):
    loudness, own = 1.0, jax.random.fold_in(rng, 6)
    for dim, parts in pieces:
        draws = jnp.exp(jax.random.uniform(jax.random.fold_in(own, dim), (parts,), jnp.float32, least / len(pieces), high / len(pieces)))
        loudness = loudness * jnp.repeat(draws, shape[dim] // parts).reshape([-1 if axis == dim else 1 for axis in range(len(shape))])
    return loudness


def bell_draw(own_key, extent, scale, limit, cuts=(), kind=jnp.bfloat16):
    array = scale * jax.random.normal(own_key, extent, jnp.float32)
    if cuts:
        array = array * levels(own_key, extent, cuts, -0.22, 0.18)
    return jnp.clip(array, -limit, limit).astype(kind)


def setup_inputs(seed: int = 0) -> dict:
    keys = jax.random.split(jax.random.key(seed), 11)
    return {
        "land_rhs": bell_draw(keys[0], (3, LANDMARKS), 1.0, 6.0, ((1, 32),), jnp.float32),
        "key_rhs": bell_draw(keys[1], (SDIM, STATES), 1.0, 6.0, ((1, 32),), jnp.float32),
        "land_damp": jnp.clip(jnp.exp(math.log(2.0) - 1.3862944 * jax.random.uniform(keys[2], (3, LANDMARKS), jnp.float32) ** levels(keys[2], (3, LANDMARKS), ((1, 32),), -0.2, 0.2)), 0.5, 2.0),
        "key_damp": jnp.clip(jnp.exp(math.log(2.0) - 1.3862944 * jax.random.uniform(keys[3], (SDIM, STATES), jnp.float32) ** levels(keys[3], (SDIM, STATES), ((1, 32),), -0.2, 0.2)), 0.5, 2.0),
        "land_jac": bell_draw(keys[4], (6, OBS), 0.3, 4.0, ((1, 32),), jnp.float32),
        "key_jac": bell_draw(keys[5], (2 * SDIM, OBS), 0.1, 1.5, ((1, 32),), jnp.float32),
        "obs_landmark": draw_obs_landmark(jax.random.fold_in(keys[10], 71), 0),
        "obs_keyframe": draw_obs_keyframe(jax.random.fold_in(keys[10], 71), 0),
        "live_blocks": draw_live_blocks(jax.random.fold_in(keys[10], 71), 0),
        "preint": draw_preint(jax.random.fold_in(keys[10], 71), 0),
    }


def window_product(preint, vectors):
    windows = preint.shape[1] // WPAR
    blocks = preint.reshape(WPAR, windows, WPAR)
    stacked = vectors.reshape(SDIM, windows, WSTATES).transpose(1, 2, 0).reshape(windows, WPAR)
    mapped = jnp.einsum("awb,wb->wa", blocks, stacked, precision=lax.Precision.HIGHEST)
    return mapped.reshape(windows, WSTATES, SDIM).transpose(2, 0, 1).reshape(SDIM, windows * WSTATES)


def normal_product(dir_land, dir_key, land_jac, key_jac, obs_landmark, obs_keyframe, validity, preint, land_damp, key_damp):
    count = land_jac.shape[1]
    land_rows = land_jac.reshape(2, 3, count)
    key_rows = key_jac.reshape(2, SDIM, count)
    seen_land = dir_land[:, obs_landmark]
    seen_key = dir_key[:, obs_keyframe]
    image = jnp.sum(land_rows * seen_land[None], axis=1) + jnp.sum(key_rows * seen_key[None], axis=1)
    image = image * validity[None]
    back_land = jnp.sum(land_rows * image[:, None], axis=0)
    back_key = jnp.sum(key_rows * image[:, None], axis=0)
    prod_land = jnp.zeros_like(dir_land).at[:, obs_landmark].add(back_land) + land_damp * dir_land
    prod_key = jnp.zeros_like(dir_key).at[:, obs_keyframe].add(back_key) + key_damp * dir_key + window_product(preint, dir_key)
    return prod_land, prod_key


def reference(land_rhs, key_rhs, land_damp, key_damp, land_jac, key_jac, obs_landmark, obs_keyframe, live_blocks, preint):
    per_device = OBLK * BLOCK
    row_ids = jnp.arange(land_jac.shape[1], dtype=jnp.int32)
    owner = row_ids // per_device
    block_ids = (row_ids % per_device) // BLOCK
    validity = (block_ids < live_blocks[owner]).astype(jnp.float32)
    landmark = ((owner // KF_GROUPS) * (KF_GROUPS * LDEV) + obs_landmark).astype(jnp.int32)
    sol_land = jnp.zeros_like(land_rhs)
    sol_key = jnp.zeros_like(key_rhs)
    res_land, res_key = land_rhs, key_rhs
    dir_land, dir_key = land_rhs, key_rhs
    norm_now = jnp.sum(res_land * res_land) + jnp.sum(res_key * res_key)
    for iteration in range(ITERS):
        prod_land, prod_key = normal_product(dir_land, dir_key, land_jac, key_jac, landmark, obs_keyframe, validity, preint, land_damp, key_damp)
        step_size = norm_now / (jnp.sum(dir_land * prod_land) + jnp.sum(dir_key * prod_key))
        sol_land = sol_land + step_size * dir_land
        sol_key = sol_key + step_size * dir_key
        res_land = res_land - step_size * prod_land
        res_key = res_key - step_size * prod_key
        norm_next = jnp.sum(res_land * res_land) + jnp.sum(res_key * res_key)
        dir_land = res_land + (norm_next / norm_now) * dir_land
        dir_key = res_key + (norm_next / norm_now) * dir_key
        norm_now = norm_next
    return sol_land, sol_key
```

```python
import functools
import jax
import jax.numpy as jnp
from jax import lax
from jax.experimental import pallas as pl
from jax.experimental.pallas import tpu as pltpu
from jax.sharding import PartitionSpec as P

WSTATES = 16
SDIM = 15
BLOCK = 128
ITERS = 2
WPAR = 240
LOW = 256
CHUNK = 1024
F32 = jnp.float32
BF16 = jnp.bfloat16


def halves(value):
    high = value.astype(BF16).astype(F32)
    return high, value - high


def stacked_halves(value):
    high, low = halves(value)
    return jnp.concatenate([high.astype(BF16), low.astype(BF16)], axis=0)


def observe_kernel(
    live_ref, lt_ref, kt_ref, lj_ref, kj_ref, il_ref, ik_ref, ol_ref, ok_ref,
    lhl_ref, khl_ref, kjp_ref, lacc_ref, kacc_ref, lplace_ref, kplace_ref,
):
    land_rows = lt_ref.shape[0]
    key_rows = kt_ref.shape[0]
    groups = land_rows // 48
    highs = key_rows // 16
    total = il_ref.shape[1]
    span = CHUNK
    limit = live_ref[0] * BLOCK
    lhl_ref[...] = stacked_halves(lt_ref[...])
    khl_ref[...] = stacked_halves(kt_ref[...])
    lacc_ref[...] = jnp.zeros_like(lacc_ref)
    kacc_ref[...] = jnp.zeros_like(kacc_ref)
    kjp_ref[...] = jnp.zeros_like(kjp_ref)

    def turn(index, carry):
        start = pl.multiple_of(index * span, span)
        cols = pl.ds(start, span)
        kjp_ref[0:SDIM, :] = kj_ref[0:SDIM, cols]
        kjp_ref[16 : 16 + SDIM, :] = kj_ref[SDIM : 2 * SDIM, cols]
        lpos = il_ref[:, cols]
        kpos = ik_ref[:, cols]
        lhigh = lpos // LOW
        khigh = kpos // LOW
        low_iota = lax.broadcasted_iota(jnp.int32, (LOW, span), 0)
        lhot = jnp.where(low_iota == lpos % LOW, 1.0, 0.0).astype(BF16)
        khot = jnp.where(low_iota == kpos % LOW, 1.0, 0.0).astype(BF16)
        lall = jnp.dot(lhl_ref[...], lhot, preferred_element_type=F32)
        kall = jnp.dot(khl_ref[...], khot, preferred_element_type=F32)
        high_iota = lax.broadcasted_iota(jnp.int32, (16, span), 0)
        lmask = [lhigh - 16 * d == high_iota for d in range(groups)]
        kmask = [jnp.broadcast_to(khigh, (16, span)) == h for h in range(highs)]
        seen_land = []
        for c in range(3):
            part = jnp.zeros((16, span), F32)
            for d in range(groups):
                row = d * 48 + c * 16
                both = lall[row : row + 16] + lall[land_rows + row : land_rows + row + 16]
                part = jnp.where(lmask[d], both, part)
            seen_land.append(jnp.sum(part, axis=0, keepdims=True))
        seen_key = jnp.zeros((16, span), F32)
        for h in range(highs):
            both = kall[h * 16 : h * 16 + 16] + kall[key_rows + h * 16 : key_rows + h * 16 + 16]
            seen_key = jnp.where(kmask[h], both, seen_key)
        inside = start + lax.broadcasted_iota(jnp.int32, (1, span), 1) < limit
        image = []
        for r in range(2):
            value = jnp.sum(kjp_ref[r * 16 : r * 16 + 16, :] * seen_key, axis=0, keepdims=True)
            for c in range(3):
                value = value + lj_ref[r * 3 + c : r * 3 + c + 1, cols] * seen_land[c]
            image.append(jnp.where(inside, value, 0.0))
        for c in range(3):
            back = (
                lj_ref[c : c + 1, cols] * image[0] + lj_ref[3 + c : 4 + c, cols] * image[1]
            )
            for p, part in enumerate(halves(back)):
                part = jnp.broadcast_to(part, (16, span))
                for d in range(groups):
                    row = p * land_rows + d * 48 + c * 16
                    lplace_ref[row : row + 16, :] = jnp.where(lmask[d], part, 0.0).astype(BF16)
        back = kjp_ref[0:16, :] * image[0] + kjp_ref[16:32, :] * image[1]
        for p, part in enumerate(halves(back)):
            for h in range(highs):
                row = p * key_rows + h * 16
                kplace_ref[row : row + 16, :] = jnp.where(kmask[h], part, 0.0).astype(BF16)
        contract = (((1,), (1,)), ((), ()))
        lacc_ref[...] += lax.dot_general(
            lplace_ref[...], lhot, contract, preferred_element_type=F32
        )
        kacc_ref[...] += lax.dot_general(
            kplace_ref[...], khot, contract, preferred_element_type=F32
        )
        return carry

    lax.fori_loop(0, total // span, turn, 0)
    ol_ref[...] = lacc_ref[0:land_rows, :] + lacc_ref[land_rows:, :]
    ok_ref[...] = kacc_ref[0:key_rows, :] + kacc_ref[key_rows:, :]


def observe(live, land_table, key_table, land_jac, key_jac, land_pos, key_pos):
    land_rows, key_rows = land_table.shape[0], key_table.shape[0]
    vmem = pl.BlockSpec(memory_space=pltpu.VMEM)
    return pl.pallas_call(
        observe_kernel,
        out_shape=(
            jax.ShapeDtypeStruct((land_rows, LOW), F32),
            jax.ShapeDtypeStruct((key_rows, LOW), F32),
        ),
        in_specs=[pl.BlockSpec(memory_space=pltpu.SMEM)] + [vmem] * 6,
        out_specs=(vmem, vmem),
        scratch_shapes=[
            pltpu.VMEM((2 * land_rows, LOW), BF16),
            pltpu.VMEM((2 * key_rows, LOW), BF16),
            pltpu.VMEM((32, CHUNK), F32),
            pltpu.VMEM((2 * land_rows, LOW), F32),
            pltpu.VMEM((2 * key_rows, LOW), F32),
            pltpu.VMEM((2 * land_rows, CHUNK), BF16),
            pltpu.VMEM((2 * key_rows, CHUNK), BF16),
        ],
        compiler_params=pltpu.CompilerParams(vmem_limit_bytes=50 * 2**20),
    )(live, land_table, key_table, land_jac, key_jac, land_pos, key_pos)


def window_kernel(pre_ref, dir_ref, out_ref, ex_ref, y_ref):
    width = pre_ref.shape[1]
    windows = width // WPAR
    states = windows * WSTATES
    for t in range(WSTATES):
        for h in range(states // LOW):
            ex_ref[t * SDIM : (t + 1) * SDIM, h * LOW : (h + 1) * LOW] = dir_ref[
                h * 16 : h * 16 + SDIM, :
            ]
    rows = lax.broadcasted_iota(jnp.int32, (WPAR, states), 0)
    cols = lax.broadcasted_iota(jnp.int32, (WPAR, states), 1)
    own_time = rows // SDIM == cols % WSTATES
    group = jnp.where(
        lax.broadcasted_iota(jnp.int32, (windows, states), 1) // WSTATES
        == lax.broadcasted_iota(jnp.int32, (windows, states), 0),
        1.0,
        0.0,
    ).astype(BF16)
    placed = jnp.where(own_time, ex_ref[...], 0.0)
    parts = [
        lax.dot_general(
            group, part.astype(BF16), (((1,), (1,)), ((), ())), preferred_element_type=F32
        ).astype(BF16)
        for part in halves(placed)
    ]
    both = jnp.concatenate(parts, axis=0)
    step = 768
    for start in range(0, width, step):
        high, low = halves(pre_ref[:, start : start + step])
        first = jnp.dot(both, high.astype(BF16), preferred_element_type=F32)
        second = jnp.dot(parts[0], low.astype(BF16), preferred_element_type=F32)
        y_ref[:, start : start + step] = first[:windows] + first[windows:] + second
    y_ref[:, width:] = jnp.zeros((windows, y_ref.shape[1] - width), F32)
    own_row = lax.broadcasted_iota(jnp.int32, (8, LOW), 0)
    strips = []
    for tile in range(windows // 8):
        strip = jnp.zeros((8, LOW), F32)
        for r in range(8):
            begin = (tile * 8 + r) * WPAR
            base = begin // 128 * 128
            block = y_ref[tile * 8 : tile * 8 + 8, base : base + 384]
            if begin != base:
                block = pltpu.roll(block, 384 - (begin - base), 1)
            strip = jnp.where(own_row == r, block[:, :LOW], strip)
        strips.append(strip)
    mapped = jnp.concatenate(strips, axis=0).T[:WPAR]
    spread = jnp.zeros((WPAR, states), F32)
    for part in halves(mapped):
        spread = spread + jnp.dot(part.astype(BF16), group, preferred_element_type=F32)
    ex_ref[...] = jnp.where(own_time, spread, 0.0)
    result = ex_ref[0:SDIM, :]
    for t in range(1, WSTATES):
        result = result + ex_ref[t * SDIM : (t + 1) * SDIM, :]
    out_ref[...] = jnp.zeros_like(out_ref)
    for h in range(states // LOW):
        out_ref[h * 16 : h * 16 + SDIM, :] = result[:, h * LOW : (h + 1) * LOW]


def window_product(preint, direction):
    windows = preint.shape[1] // WPAR
    vmem = pl.BlockSpec(memory_space=pltpu.VMEM)
    return pl.pallas_call(
        window_kernel,
        out_shape=jax.ShapeDtypeStruct(direction.shape, F32),
        in_specs=[vmem, vmem],
        out_specs=vmem,
        scratch_shapes=[
            pltpu.VMEM((WPAR, windows * WSTATES), F32),
            pltpu.VMEM((windows, preint.shape[1] + 384), F32),
        ],
        compiler_params=pltpu.CompilerParams(vmem_limit_bytes=50 * 2**20),
    )(preint, direction)


def fold_key(array):
    states = array.shape[1]
    parts = array.reshape(SDIM, states // LOW, LOW).transpose(1, 0, 2)
    return jnp.pad(parts, ((0, 0), (0, 1), (0, 0))).reshape(-1, LOW)


def unfold_key(array):
    parts = array.reshape(-1, 16, LOW)[:, :SDIM].transpose(1, 0, 2)
    return parts.reshape(SDIM, -1)


def shards(
    land_rhs, key_rhs, land_damp, key_damp, land_jac, key_jac,
    obs_landmark, obs_keyframe, live_blocks, preint,
):
    state_dev = key_rhs.shape[1]
    kf_count = lax.axis_size("kf")
    key_pos = obs_keyframe // state_dev // kf_count * state_dev + obs_keyframe % state_dev
    key_pos = key_pos[None]
    land_pos = obs_landmark[None]
    land_shape = land_rhs.shape
    res_land = land_rhs.reshape(-1, LOW)
    damp_land = land_damp.reshape(-1, LOW)
    res_key = fold_key(key_rhs)
    damp_key = fold_key(key_damp)
    both = ("lm", "kf")

    def inner(a_land, b_land, a_key, b_key):
        return jnp.sum(a_land * b_land) + jnp.sum(a_key * b_key)

    dir_land, dir_key = res_land, res_key
    sol_land = jnp.zeros_like(res_land)
    sol_key = jnp.zeros_like(res_key)
    norm_now = lax.psum(inner(res_land, res_land, res_key, res_key), both)
    for iteration in range(ITERS):
        land_table = lax.all_gather(dir_land, "kf", axis=0, tiled=True)
        key_table = lax.all_gather(dir_key, "lm", axis=0, tiled=True)
        window = window_product(preint, dir_key)
        sum_land, sum_key = observe(
            live_blocks, land_table, key_table, land_jac, key_jac, land_pos, key_pos
        )
        prod_land = lax.psum_scatter(sum_land, "kf", scatter_dimension=0, tiled=True)
        prod_key = lax.psum_scatter(sum_key, "lm", scatter_dimension=0, tiled=True)
        prod_land = prod_land + damp_land * dir_land
        prod_key = prod_key + damp_key * dir_key + window
        step_size = norm_now / lax.psum(inner(dir_land, prod_land, dir_key, prod_key), both)
        sol_land = sol_land + step_size * dir_land
        sol_key = sol_key + step_size * dir_key
        if iteration == ITERS - 1:
            break
        res_land = res_land - step_size * prod_land
        res_key = res_key - step_size * prod_key
        norm_next = lax.psum(inner(res_land, res_land, res_key, res_key), both)
        dir_land = res_land + norm_next / norm_now * dir_land
        dir_key = res_key + norm_next / norm_now * dir_key
        norm_now = norm_next
    return sol_land.reshape(land_shape), unfold_key(sol_key)


def solution(mesh):
    split = P(None, ("lm", "kf"))
    line = P(("lm", "kf"))
    in_specs = (split,) * 6 + (line, line, line, split)
    return jax.shard_map(
        shards, mesh=mesh, in_specs=in_specs, out_specs=(split, split), check_vma=False
    )
```

```python
import jax
import jax.numpy as jnp
from jax import lax
from jax.experimental import pallas as pl
from jax.experimental.pallas import tpu as pltpu
from jax.sharding import PartitionSpec as P

WSTATES = 16
SDIM = 15
BLOCK = 128
WPAR = 240
LOW = 256
CHUNK = 1024
F32 = jnp.float32
BF16 = jnp.bfloat16


def halves(value):
    high = value.astype(BF16).astype(F32)
    return high, value - high


def stacked_halves(value):
    high, low = halves(value)
    return jnp.concatenate([high.astype(BF16), low.astype(BF16)], axis=0)


def observe_kernel(
    live_ref, lt_ref, kt_ref, lj_ref, kj_ref, il_ref, ik_ref, ol_ref, ok_ref,
    lhl_ref, khl_ref, kjp_ref, lacc_ref, kacc_ref, lplace_ref, kplace_ref,
):
    land_rows = lt_ref.shape[0]
    key_rows = kt_ref.shape[0]
    groups = land_rows // 48
    highs = key_rows // 16
    total = il_ref.shape[1]
    span = CHUNK
    limit = live_ref[0] * BLOCK
    lhl_ref[...] = stacked_halves(lt_ref[...])
    khl_ref[...] = stacked_halves(kt_ref[...])
    lacc_ref[...] = jnp.zeros_like(lacc_ref)
    kacc_ref[...] = jnp.zeros_like(kacc_ref)
    kjp_ref[...] = jnp.zeros_like(kjp_ref)

    def turn(index, carry):
        start = pl.multiple_of(index * span, span)
        cols = pl.ds(start, span)
        kjp_ref[0:SDIM, :] = kj_ref[0:SDIM, cols]
        kjp_ref[16 : 16 + SDIM, :] = kj_ref[SDIM : 2 * SDIM, cols]
        lpos = il_ref[:, cols]
        kpos = ik_ref[:, cols]
        lhigh = lpos // LOW
        khigh = kpos // LOW
        low_iota = lax.broadcasted_iota(jnp.int32, (LOW, span), 0)
        lhot = jnp.where(low_iota == lpos % LOW, 1.0, 0.0).astype(BF16)
        khot = jnp.where(low_iota == kpos % LOW, 1.0, 0.0).astype(BF16)
        lall = jnp.dot(lhl_ref[...], lhot, preferred_element_type=F32)
        kall = jnp.dot(khl_ref[...], khot, preferred_element_type=F32)
        high_iota = lax.broadcasted_iota(jnp.int32, (16, span), 0)
        lmask = [lhigh - 16 * d == high_iota for d in range(groups)]
        kmask = [jnp.broadcast_to(khigh, (16, span)) == h for h in range(highs)]
        seen_land = []
        for c in range(3):
            part = jnp.zeros((16, span), F32)
            for d in range(groups):
                row = d * 48 + c * 16
                both = lall[row : row + 16] + lall[land_rows + row : land_rows + row + 16]
                part = jnp.where(lmask[d], both, part)
            seen_land.append(jnp.sum(part, axis=0, keepdims=True))
        seen_key = jnp.zeros((16, span), F32)
        for h in range(highs):
            both = kall[h * 16 : h * 16 + 16] + kall[key_rows + h * 16 : key_rows + h * 16 + 16]
            seen_key = jnp.where(kmask[h], both, seen_key)
        inside = start + lax.broadcasted_iota(jnp.int32, (1, span), 1) < limit
        image = []
        for r in range(2):
            value = jnp.sum(kjp_ref[r * 16 : r * 16 + 16, :] * seen_key, axis=0, keepdims=True)
            for c in range(3):
                value = value + lj_ref[r * 3 + c : r * 3 + c + 1, cols] * seen_land[c]
            image.append(jnp.where(inside, value, 0.0))
        for c in range(3):
            back = (
                lj_ref[c : c + 1, cols] * image[0] + lj_ref[3 + c : 4 + c, cols] * image[1]
            )
            for p, part in enumerate(halves(back)):
                part = jnp.broadcast_to(part, (16, span))
                for d in range(groups):
                    row = p * land_rows + d * 48 + c * 16
                    lplace_ref[row : row + 16, :] = jnp.where(lmask[d], part, 0.0).astype(BF16)
        back = kjp_ref[0:16, :] * image[0] + kjp_ref[16:32, :] * image[1]
        for p, part in enumerate(halves(back)):
            for h in range(highs):
                row = p * key_rows + h * 16
                kplace_ref[row : row + 16, :] = jnp.where(kmask[h], part, 0.0).astype(BF16)
        contract = (((1,), (1,)), ((), ()))
        lacc_ref[...] += lax.dot_general(
            lplace_ref[...], lhot, contract, preferred_element_type=F32
        )
        kacc_ref[...] += lax.dot_general(
            kplace_ref[...], khot, contract, preferred_element_type=F32
        )
        return carry

    lax.fori_loop(0, total // span, turn, 0)
    ol_ref[...] = lacc_ref[0:land_rows, :] + lacc_ref[land_rows:, :]
    ok_ref[...] = kacc_ref[0:key_rows, :] + kacc_ref[key_rows:, :]


def observe(live, land_table, key_table, land_jac, key_jac, land_pos, key_pos):
    land_rows, key_rows = land_table.shape[0], key_table.shape[0]
    vmem = pl.BlockSpec(memory_space=pltpu.VMEM)
    return pl.pallas_call(
        observe_kernel,
        out_shape=(
            jax.ShapeDtypeStruct((land_rows, LOW), F32),
            jax.ShapeDtypeStruct((key_rows, LOW), F32),
        ),
        in_specs=[pl.BlockSpec(memory_space=pltpu.SMEM)] + [vmem] * 6,
        out_specs=(vmem, vmem),
        scratch_shapes=[
            pltpu.VMEM((2 * land_rows, LOW), BF16),
            pltpu.VMEM((2 * key_rows, LOW), BF16),
            pltpu.VMEM((32, CHUNK), F32),
            pltpu.VMEM((2 * land_rows, LOW), F32),
            pltpu.VMEM((2 * key_rows, LOW), F32),
            pltpu.VMEM((2 * land_rows, CHUNK), BF16),
            pltpu.VMEM((2 * key_rows, CHUNK), BF16),
        ],
        compiler_params=pltpu.CompilerParams(vmem_limit_bytes=50 * 2**20),
    )(live, land_table, key_table, land_jac, key_jac, land_pos, key_pos)


def window_kernel(pre_ref, dir_ref, out_ref, ex_ref, y_ref):
    width = pre_ref.shape[1]
    windows = width // WPAR
    states = windows * WSTATES
    for t in range(WSTATES):
        for h in range(states // LOW):
            ex_ref[t * SDIM : (t + 1) * SDIM, h * LOW : (h + 1) * LOW] = dir_ref[
                h * 16 : h * 16 + SDIM, :
            ]
    rows = lax.broadcasted_iota(jnp.int32, (WPAR, states), 0)
    cols = lax.broadcasted_iota(jnp.int32, (WPAR, states), 1)
    own_time = rows // SDIM == cols % WSTATES
    group = jnp.where(
        lax.broadcasted_iota(jnp.int32, (windows, states), 1) // WSTATES
        == lax.broadcasted_iota(jnp.int32, (windows, states), 0),
        1.0,
        0.0,
    ).astype(BF16)
    placed = jnp.where(own_time, ex_ref[...], 0.0)
    parts = [
        lax.dot_general(
            group, part.astype(BF16), (((1,), (1,)), ((), ())), preferred_element_type=F32
        ).astype(BF16)
        for part in halves(placed)
    ]
    both = jnp.concatenate(parts, axis=0)
    step = 768
    for start in range(0, width, step):
        high, low = halves(pre_ref[:, start : start + step])
        first = jnp.dot(both, high.astype(BF16), preferred_element_type=F32)
        second = jnp.dot(parts[0], low.astype(BF16), preferred_element_type=F32)
        y_ref[:, start : start + step] = first[:windows] + first[windows:] + second
    y_ref[:, width:] = jnp.zeros((windows, y_ref.shape[1] - width), F32)
    own_row = lax.broadcasted_iota(jnp.int32, (8, LOW), 0)
    strips = []
    for tile in range(windows // 8):
        strip = jnp.zeros((8, LOW), F32)
        for r in range(8):
            begin = (tile * 8 + r) * WPAR
            base = begin // 128 * 128
            block = y_ref[tile * 8 : tile * 8 + 8, base : base + 384]
            if begin != base:
                block = pltpu.roll(block, 384 - (begin - base), 1)
            strip = jnp.where(own_row == r, block[:, :LOW], strip)
        strips.append(strip)
    mapped = jnp.concatenate(strips, axis=0).T[:WPAR]
    spread = jnp.zeros((WPAR, states), F32)
    for part in halves(mapped):
        spread = spread + jnp.dot(part.astype(BF16), group, preferred_element_type=F32)
    ex_ref[...] = jnp.where(own_time, spread, 0.0)
    result = ex_ref[0:SDIM, :]
    for t in range(1, WSTATES):
        result = result + ex_ref[t * SDIM : (t + 1) * SDIM, :]
    out_ref[...] = jnp.zeros_like(out_ref)
    for h in range(states // LOW):
        out_ref[h * 16 : h * 16 + SDIM, :] = result[:, h * LOW : (h + 1) * LOW]


def window_product(preint, direction):
    windows = preint.shape[1] // WPAR
    vmem = pl.BlockSpec(memory_space=pltpu.VMEM)
    return pl.pallas_call(
        window_kernel,
        out_shape=jax.ShapeDtypeStruct(direction.shape, F32),
        in_specs=[vmem, vmem],
        out_specs=vmem,
        scratch_shapes=[
            pltpu.VMEM((WPAR, windows * WSTATES), F32),
            pltpu.VMEM((windows, preint.shape[1] + 384), F32),
        ],
        compiler_params=pltpu.CompilerParams(vmem_limit_bytes=50 * 2**20),
    )(preint, direction)


def fold_key(array):
    states = array.shape[1]
    parts = array.reshape(SDIM, states // LOW, LOW).transpose(1, 0, 2)
    return jnp.pad(parts, ((0, 0), (0, 1), (0, 0))).reshape(-1, LOW)


def unfold_key(array):
    parts = array.reshape(-1, 16, LOW)[:, :SDIM].transpose(1, 0, 2)
    return parts.reshape(SDIM, -1)


def greet():
    barrier = pltpu.get_barrier_semaphore()
    count = 0
    for axis in ("lm", "kf"):
        size = lax.axis_size(axis)
        place = lax.axis_index(axis)
        for hop in range(1, size):
            pl.semaphore_signal(
                barrier,
                inc=1,
                device_id={axis: lax.rem(place + hop, size)},
                device_id_type=pl.DeviceIdType.MESH,
            )
            count += 1
    pl.semaphore_wait(barrier, count)


def send(axis, source, target, sems):
    size = lax.axis_size(axis)
    place = lax.axis_index(axis)
    copies = []
    for hop in range(1, size):
        peer = lax.rem(place + hop, size)
        copy = pltpu.make_async_remote_copy(
            src_ref=source(peer, hop),
            dst_ref=target(peer, hop),
            send_sem=sems.at[0, hop - 1],
            recv_sem=sems.at[1, hop - 1],
            device_id={axis: peer},
            device_id_type=pl.DeviceIdType.MESH,
        )
        copy.start()
        copies.append(copy)
    return copies


def finish(copies):
    for copy in copies:
        copy.wait()


def gather_start(axis, table, sems):
    place = lax.axis_index(axis)
    mine = table.at[place]
    return send(axis, lambda peer, hop: mine, lambda peer, hop: mine, sems)


def scatter_start(axis, parts, slots, sems):
    return send(
        axis, lambda peer, hop: parts.at[peer], lambda peer, hop: slots.at[hop - 1], sems
    )


def scatter_total(axis, parts, slots):
    total = parts[lax.axis_index(axis)]
    for hop in range(1, lax.axis_size(axis)):
        total = total + slots[hop - 1]
    return total


def sum_all(tile, kf_slots, lm_slots, kf_sems, lm_sems):
    for axis, slots, sems in (("kf", kf_slots, kf_sems), ("lm", lm_slots, lm_sems)):
        slots[lax.axis_index(axis)] = tile
        finish(gather_start(axis, slots, sems))
        tile = slots[0]
        for place in range(1, lax.axis_size(axis)):
            tile = tile + slots[place]
    return tile


def inner(a_land, b_land, a_key, b_key):
    return jnp.sum(a_land * b_land, keepdims=True) + jnp.sum(a_key * b_key, keepdims=True)


def two_rows(first, second):
    rows = lax.broadcasted_iota(jnp.int32, (8, 128), 0)
    return jnp.where(rows == 0, first, second)


def gather_kernel(land_ref, key_ref, lt_ref, kt_ref, lsems, ksems):
    greet()
    lt_ref[lax.axis_index("kf")] = land_ref[...]
    kt_ref[lax.axis_index("lm")] = key_ref[...]
    copies = gather_start("kf", lt_ref, lsems) + gather_start("lm", kt_ref, ksems)
    finish(copies)


def step_kernel(
    sl_ref, sk_ref, lt_ref, kt_ref, ld_ref, kd_ref, win_ref,
    rl_ref, rk_ref, own_ref, ql_ref, qk_ref, scal_ref,
    lslots, kslots, kf_slots, lm_slots, lsems, ksems, lgs, kgs, kfs, lms,
):
    greet()
    kf_place = lax.axis_index("kf")
    lm_place = lax.axis_index("lm")
    copies = scatter_start("kf", sl_ref, lslots, lsems)
    copies += scatter_start("lm", sk_ref, kslots, ksems)
    dir_land = lt_ref[kf_place]
    dir_key = kt_ref[lm_place]
    norm = inner(dir_land, dir_land, dir_key, dir_key)
    finish(copies)
    prod_land = scatter_total("kf", sl_ref, lslots) + ld_ref[...] * dir_land
    prod_key = scatter_total("lm", sk_ref, kslots) + kd_ref[...] * dir_key + win_ref[...]
    rl_ref[kf_place] = prod_land
    rk_ref[lm_place] = prod_key
    copies = gather_start("kf", rl_ref, lgs) + gather_start("lm", rk_ref, kgs)
    ql_ref[...] = prod_land
    qk_ref[...] = prod_key
    tile = two_rows(norm, inner(dir_land, prod_land, dir_key, prod_key))
    tile = sum_all(tile, kf_slots, lm_slots, kfs, lms)
    norm = tile[0:1, 0:1]
    step = norm / tile[1:2, 0:1]
    scal_ref[...] = two_rows(norm, step)
    own_ref[...] = dir_key - step * prod_key
    finish(copies)
    rl_ref[...] = lt_ref[...] - step[None] * rl_ref[...]
    rk_ref[...] = kt_ref[...] - step[None] * rk_ref[...]


def last_kernel(
    sl_ref, sk_ref, dl_ref, dk_ref, ql_ref, qk_ref, ld_ref, kd_ref, win_ref, scal_ref,
    ol_ref, ok_ref,
    lslots, kslots, kf_slots, lm_slots, kf_more, lm_more, lsems, ksems, kfs, lms, kft, lmt,
):
    greet()
    copies = scatter_start("kf", sl_ref, lslots, lsems)
    copies += scatter_start("lm", sk_ref, kslots, ksems)
    norm = scal_ref[0:1, 0:1]
    step = scal_ref[1:2, 0:1]
    old_land, old_key = dl_ref[...], dk_ref[...]
    prod_land, prod_key = ql_ref[...], qk_ref[...]
    res_land = old_land - step * prod_land
    res_key = old_key - step * prod_key
    part = inner(res_land, res_land, res_key, res_key)
    tile = sum_all(two_rows(part, part), kf_slots, lm_slots, kfs, lms)
    norm_next = tile[0:1, 0:1]
    beta = norm_next / norm
    dir_land = res_land + beta * old_land
    dir_key = res_key + beta * old_key
    finish(copies)
    new_land = scatter_total("kf", sl_ref, lslots) + ld_ref[...] * res_land
    new_key = scatter_total("lm", sk_ref, kslots) + kd_ref[...] * res_key + win_ref[...]
    new_land = new_land + beta * prod_land
    new_key = new_key + beta * prod_key
    part = inner(dir_land, new_land, dir_key, new_key)
    tile = sum_all(two_rows(part, part), kf_more, lm_more, kft, lmt)
    next_step = norm_next / tile[0:1, 0:1]
    ol_ref[...] = step * old_land + next_step * dir_land
    ok_ref[...] = step * old_key + next_step * dir_key


def exchange(kernel, identity, outs, scratch, *operands):
    vmem = pl.BlockSpec(memory_space=pltpu.VMEM)
    return pl.pallas_call(
        kernel,
        out_shape=tuple(jax.ShapeDtypeStruct(shape, F32) for shape in outs),
        in_specs=[vmem] * len(operands),
        out_specs=(vmem,) * len(outs),
        scratch_shapes=scratch,
        compiler_params=pltpu.CompilerParams(
            collective_id=identity, has_side_effects=True, vmem_limit_bytes=16 * 2**20
        ),
    )(*operands)


def shards(
    land_rhs, key_rhs, land_damp, key_damp, land_jac, key_jac,
    obs_landmark, obs_keyframe, live_blocks, preint,
):
    state_dev = key_rhs.shape[1]
    kf_count = lax.axis_size("kf")
    lm_count = lax.axis_size("lm")
    key_pos = obs_keyframe // state_dev // kf_count * state_dev + obs_keyframe % state_dev
    key_pos = key_pos[None]
    land_pos = obs_landmark[None]
    land_shape = land_rhs.shape
    dir_land = land_rhs.reshape(-1, LOW)
    damp_land = land_damp.reshape(-1, LOW)
    dir_key = fold_key(key_rhs)
    damp_key = fold_key(key_damp)
    own_land, own_key = dir_land.shape, dir_key.shape
    all_land, all_key = (kf_count,) + own_land, (lm_count,) + own_key

    kf_sems = pltpu.SemaphoreType.DMA((2, kf_count - 1))
    lm_sems = pltpu.SemaphoreType.DMA((2, lm_count - 1))
    slots = [
        pltpu.VMEM((kf_count - 1,) + own_land, F32),
        pltpu.VMEM((lm_count - 1,) + own_key, F32),
    ]
    tiles = [pltpu.VMEM((kf_count, 8, 128), F32), pltpu.VMEM((lm_count, 8, 128), F32)]
    sems = [kf_sems, lm_sems]

    def seen(land_table, key_table):
        land, key = observe(
            live_blocks,
            land_table.reshape(-1, LOW),
            key_table.reshape(-1, LOW),
            land_jac,
            key_jac,
            land_pos,
            key_pos,
        )
        return land.reshape(all_land), key.reshape(all_key)

    land_table, key_table = exchange(
        gather_kernel, 1, (all_land, all_key), sems, dir_land, dir_key
    )
    window = window_product(preint, dir_key)
    sum_land, sum_key = seen(land_table, key_table)
    res_land, res_key, own_res, prod_land, prod_key, scal = exchange(
        step_kernel,
        2,
        (all_land, all_key, own_key, own_land, own_key, (8, 128)),
        slots + tiles + sems * 3,
        sum_land,
        sum_key,
        land_table,
        key_table,
        damp_land,
        damp_key,
        window,
    )
    window = window_product(preint, own_res)
    sum_land, sum_key = seen(res_land, res_key)
    sol_land, sol_key = exchange(
        last_kernel,
        3,
        (own_land, own_key),
        slots + tiles * 2 + sems * 3,
        sum_land,
        sum_key,
        dir_land,
        dir_key,
        prod_land,
        prod_key,
        damp_land,
        damp_key,
        window,
        scal,
    )
    return sol_land.reshape(land_shape), unfold_key(sol_key)


def solution(mesh):
    split = P(None, ("lm", "kf"))
    line = P(("lm", "kf"))
    in_specs = (split,) * 6 + (line, line, line, split)
    return jax.shard_map(
        shards, mesh=mesh, in_specs=in_specs, out_specs=(split, split), check_vma=False
    )
```

```python
import functools
import jax
import jax.numpy as jnp
from jax import lax
from jax.experimental import pallas as pl
from jax.experimental.pallas import tpu as pltpu
from jax.sharding import PartitionSpec as P

WSTATES = 16
SDIM = 15
BLOCK = 128
WPAR = 240
LOW = 256
CHUNK = 4096
F32 = jnp.float32
BF16 = jnp.bfloat16


def halves(value):
    high = value.astype(BF16).astype(F32)
    return high, value - high


def stacked_halves(value):
    high, low = halves(value)
    return jnp.concatenate([high.astype(BF16), low.astype(BF16)], axis=0)


def observe_kernel(spread, live_ref, lt_ref, kt_ref, lj_ref, kj_ref, il_ref, ik_ref, *rest):
    if spread:
        ol_ref, ok_ref, os_ref = rest[:3]
        lhl_ref, khl_ref, kjp_ref, lacc_ref, kacc_ref, lplace_ref, kplace_ref = rest[3:]
    else:
        os_ref, lhl_ref, khl_ref, kjp_ref = rest
    land_rows = lt_ref.shape[0]
    key_rows = kt_ref.shape[0]
    groups = land_rows // 48
    highs = key_rows // 16
    total = il_ref.shape[1]
    span = CHUNK
    limit = live_ref[0] * BLOCK
    lhl_ref[...] = stacked_halves(lt_ref[...])
    khl_ref[...] = stacked_halves(kt_ref[...])
    if spread:
        lacc_ref[...] = jnp.zeros_like(lacc_ref)
        kacc_ref[...] = jnp.zeros_like(kacc_ref)
    kjp_ref[...] = jnp.zeros_like(kjp_ref)

    def turn(index, carry):
        start = pl.multiple_of(index * span, span)
        cols = pl.ds(start, span)
        kjp_ref[0:SDIM, :] = kj_ref[0:SDIM, cols]
        kjp_ref[16 : 16 + SDIM, :] = kj_ref[SDIM : 2 * SDIM, cols]
        lpos = il_ref[:, cols]
        kpos = ik_ref[:, cols]
        lhigh = lpos // LOW
        khigh = kpos // LOW
        low_iota = lax.broadcasted_iota(jnp.int32, (LOW, span), 0)
        low16 = low_iota.astype(F32).astype(BF16)
        one, zero = jnp.ones((), BF16), jnp.zeros((), BF16)
        llow = jnp.broadcast_to((lpos % LOW).astype(F32).astype(BF16), (LOW, span))
        klow = jnp.broadcast_to((kpos % LOW).astype(F32).astype(BF16), (LOW, span))
        lhot = jnp.where(low16 == llow, one, zero)
        khot = jnp.where(low16 == klow, one, zero)
        lcat = jnp.concatenate([lhl_ref[0:land_rows, :], lhl_ref[land_rows:, :]], axis=1)
        kcat = jnp.concatenate([khl_ref[0:key_rows, :], khl_ref[key_rows:, :]], axis=1)
        lall = jnp.dot(
            lcat, jnp.concatenate([lhot, lhot], axis=0), preferred_element_type=F32
        )
        kall = jnp.dot(
            kcat, jnp.concatenate([khot, khot], axis=0), preferred_element_type=F32
        )
        high_iota = lax.broadcasted_iota(jnp.int32, (16, span), 0)
        lmask = [lhigh - 16 * d == high_iota for d in range(groups)]
        kmask = [jnp.broadcast_to(khigh, (16, span)) == h for h in range(highs)]
        seen_land = []
        for c in range(3):
            part = jnp.zeros((16, span), F32)
            for d in range(groups):
                row = d * 48 + c * 16
                both = lall[row : row + 16]
                part = jnp.where(lmask[d], both, part)
            seen_land.append(jnp.sum(part, axis=0, keepdims=True))
        seen_key = jnp.zeros((16, span), F32)
        for h in range(highs):
            both = kall[h * 16 : h * 16 + 16]
            seen_key = jnp.where(kmask[h], both, seen_key)
        inside = start + lax.broadcasted_iota(jnp.int32, (1, span), 1) < limit
        image = []
        for r in range(2):
            value = jnp.sum(kjp_ref[r * 16 : r * 16 + 16, :] * seen_key, axis=0, keepdims=True)
            for c in range(3):
                value = value + lj_ref[r * 3 + c : r * 3 + c + 1, cols] * seen_land[c]
            image.append(jnp.where(inside, value, 0.0))
        carry = carry + image[0] * image[0] + image[1] * image[1]
        if not spread:
            return carry
        lplace = (lhigh - high_iota).astype(F32).astype(BF16)
        kplace = jnp.broadcast_to(khigh, (16, span)).astype(F32).astype(BF16)
        for c in range(3):
            back = (
                lj_ref[c : c + 1, cols] * image[0] + lj_ref[3 + c : 4 + c, cols] * image[1]
            )
            for p, part in enumerate(halves(back)):
                part = jnp.broadcast_to(part, (16, span)).astype(BF16)
                for d in range(groups):
                    row = p * land_rows + d * 48 + c * 16
                    here = lplace == jnp.full((), 16 * d, BF16)
                    lplace_ref[row : row + 16, :] = jnp.where(here, part, zero)
        back = kjp_ref[0:16, :] * image[0] + kjp_ref[16:32, :] * image[1]
        for p, part in enumerate(halves(back)):
            part = part.astype(BF16)
            for h in range(highs):
                row = p * key_rows + h * 16
                here = kplace == jnp.full((), h, BF16)
                kplace_ref[row : row + 16, :] = jnp.where(here, part, zero)
        contract = (((1,), (1,)), ((), ()))
        lacc_ref[...] += lax.dot_general(
            lplace_ref[...], lhot, contract, preferred_element_type=F32
        )
        kacc_ref[...] += lax.dot_general(
            kplace_ref[...], khot, contract, preferred_element_type=F32
        )
        return carry

    squares = lax.fori_loop(0, total // span, turn, jnp.zeros((1, span), F32))
    os_ref[...] = jnp.broadcast_to(jnp.sum(squares, keepdims=True), os_ref.shape)
    if spread:
        ol_ref[...] = lacc_ref[0:land_rows, :] + lacc_ref[land_rows:, :]
        ok_ref[...] = kacc_ref[0:key_rows, :] + kacc_ref[key_rows:, :]


def observe(spread, live, land_table, key_table, land_jac, key_jac, land_pos, key_pos):
    land_rows, key_rows = land_table.shape[0], key_table.shape[0]
    vmem = pl.BlockSpec(memory_space=pltpu.VMEM)
    outs = [jax.ShapeDtypeStruct((8, 128), F32)]
    scratch = [
        pltpu.VMEM((2 * land_rows, LOW), BF16),
        pltpu.VMEM((2 * key_rows, LOW), BF16),
        pltpu.VMEM((32, CHUNK), F32),
    ]
    if spread:
        outs = [
            jax.ShapeDtypeStruct((land_rows, LOW), F32),
            jax.ShapeDtypeStruct((key_rows, LOW), F32),
        ] + outs
        scratch += [
            pltpu.VMEM((2 * land_rows, LOW), F32),
            pltpu.VMEM((2 * key_rows, LOW), F32),
            pltpu.VMEM((2 * land_rows, CHUNK), BF16),
            pltpu.VMEM((2 * key_rows, CHUNK), BF16),
        ]
    return pl.pallas_call(
        functools.partial(observe_kernel, spread),
        out_shape=tuple(outs),
        in_specs=[pl.BlockSpec(memory_space=pltpu.SMEM)] + [vmem] * 6,
        out_specs=(vmem,) * len(outs),
        scratch_shapes=scratch,
        compiler_params=pltpu.CompilerParams(vmem_limit_bytes=50 * 2**20),
    )(live, land_table, key_table, land_jac, key_jac, land_pos, key_pos)


def window_kernel(pre_ref, dir_ref, out_ref, ex_ref, y_ref):
    width = pre_ref.shape[1]
    windows = width // WPAR
    states = windows * WSTATES
    for t in range(WSTATES):
        for h in range(states // LOW):
            ex_ref[t * SDIM : (t + 1) * SDIM, h * LOW : (h + 1) * LOW] = dir_ref[
                h * 16 : h * 16 + SDIM, :
            ]
    rows = lax.broadcasted_iota(jnp.int32, (WPAR, states), 0)
    cols = lax.broadcasted_iota(jnp.int32, (WPAR, states), 1)
    own_time = rows // SDIM == cols % WSTATES
    group = jnp.where(
        lax.broadcasted_iota(jnp.int32, (windows, states), 1) // WSTATES
        == lax.broadcasted_iota(jnp.int32, (windows, states), 0),
        1.0,
        0.0,
    ).astype(BF16)
    placed = jnp.where(own_time, ex_ref[...], 0.0)
    parts = [
        lax.dot_general(
            group, part.astype(BF16), (((1,), (1,)), ((), ())), preferred_element_type=F32
        ).astype(BF16)
        for part in halves(placed)
    ]
    both = jnp.concatenate(parts, axis=0)
    step = 768
    for start in range(0, width, step):
        high, low = halves(pre_ref[:, start : start + step])
        first = jnp.dot(both, high.astype(BF16), preferred_element_type=F32)
        second = jnp.dot(parts[0], low.astype(BF16), preferred_element_type=F32)
        y_ref[:, start : start + step] = first[:windows] + first[windows:] + second
    y_ref[:, width:] = jnp.zeros((windows, y_ref.shape[1] - width), F32)
    own_row = lax.broadcasted_iota(jnp.int32, (8, LOW), 0)
    strips = []
    for tile in range(windows // 8):
        strip = jnp.zeros((8, LOW), F32)
        for r in range(8):
            begin = (tile * 8 + r) * WPAR
            base = begin // 128 * 128
            block = y_ref[tile * 8 : tile * 8 + 8, base : base + 384]
            if begin != base:
                block = pltpu.roll(block, 384 - (begin - base), 1)
            strip = jnp.where(own_row == r, block[:, :LOW], strip)
        strips.append(strip)
    mapped = jnp.concatenate(strips, axis=0).T[:WPAR]
    spread = jnp.zeros((WPAR, states), F32)
    for part in halves(mapped):
        spread = spread + jnp.dot(part.astype(BF16), group, preferred_element_type=F32)
    ex_ref[...] = jnp.where(own_time, spread, 0.0)
    result = ex_ref[0:SDIM, :]
    for t in range(1, WSTATES):
        result = result + ex_ref[t * SDIM : (t + 1) * SDIM, :]
    out_ref[...] = jnp.zeros_like(out_ref)
    for h in range(states // LOW):
        out_ref[h * 16 : h * 16 + SDIM, :] = result[:, h * LOW : (h + 1) * LOW]


def window_product(preint, direction):
    windows = preint.shape[1] // WPAR
    vmem = pl.BlockSpec(memory_space=pltpu.VMEM)
    return pl.pallas_call(
        window_kernel,
        out_shape=jax.ShapeDtypeStruct(direction.shape, F32),
        in_specs=[vmem, vmem],
        out_specs=vmem,
        scratch_shapes=[
            pltpu.VMEM((WPAR, windows * WSTATES), F32),
            pltpu.VMEM((windows, preint.shape[1] + 384), F32),
        ],
        compiler_params=pltpu.CompilerParams(vmem_limit_bytes=50 * 2**20),
    )(preint, direction)


def fold_key(array):
    states = array.shape[1]
    parts = array.reshape(SDIM, states // LOW, LOW).transpose(1, 0, 2)
    return jnp.pad(parts, ((0, 0), (0, 1), (0, 0))).reshape(-1, LOW)


def unfold_key(array):
    parts = array.reshape(-1, 16, LOW)[:, :SDIM].transpose(1, 0, 2)
    return parts.reshape(SDIM, -1)


def greet():
    barrier = pltpu.get_barrier_semaphore()
    count = 0
    for axis in ("lm", "kf"):
        size = lax.axis_size(axis)
        place = lax.axis_index(axis)
        for hop in range(1, size):
            pl.semaphore_signal(
                barrier,
                inc=1,
                device_id={axis: lax.rem(place + hop, size)},
                device_id_type=pl.DeviceIdType.MESH,
            )
            count += 1
    pl.semaphore_wait(barrier, count)


def send(axis, source, target, sems):
    size = lax.axis_size(axis)
    place = lax.axis_index(axis)
    copies = []
    for hop in range(1, size):
        peer = lax.rem(place + hop, size)
        copy = pltpu.make_async_remote_copy(
            src_ref=source(peer, hop),
            dst_ref=target(peer, hop),
            send_sem=sems.at[0, hop - 1],
            recv_sem=sems.at[1, hop - 1],
            device_id={axis: peer},
            device_id_type=pl.DeviceIdType.MESH,
        )
        copy.start()
        copies.append(copy)
    return copies


def finish(copies):
    for copy in copies:
        copy.wait()


def gather_start(axis, table, sems):
    place = lax.axis_index(axis)
    mine = table.at[place]
    return send(axis, lambda peer, hop: mine, lambda peer, hop: mine, sems)


def scatter_start(axis, parts, slots, sems):
    return send(
        axis, lambda peer, hop: parts.at[peer], lambda peer, hop: slots.at[hop - 1], sems
    )


def scatter_total(axis, parts, slots):
    total = parts[lax.axis_index(axis)]
    for hop in range(1, lax.axis_size(axis)):
        total = total + slots[hop - 1]
    return total


def sum_all(tile, kf_slots, lm_slots, kf_sems, lm_sems):
    for axis, slots, sems in (("kf", kf_slots, kf_sems), ("lm", lm_slots, lm_sems)):
        slots[lax.axis_index(axis)] = tile
        finish(gather_start(axis, slots, sems))
        tile = slots[0]
        for place in range(1, lax.axis_size(axis)):
            tile = tile + slots[place]
    return tile


def inner(a_land, b_land, a_key, b_key):
    return jnp.sum(a_land * b_land, keepdims=True) + jnp.sum(a_key * b_key, keepdims=True)


def three_rows(first, second, third):
    rows = lax.broadcasted_iota(jnp.int32, (8, 128), 0)
    return jnp.where(rows == 0, first, jnp.where(rows == 1, second, third))


def gather_kernel(land_ref, key_ref, lt_ref, kt_ref, lsems, ksems):
    greet()
    lt_ref[lax.axis_index("kf")] = land_ref[...]
    kt_ref[lax.axis_index("lm")] = key_ref[...]
    copies = gather_start("kf", lt_ref, lsems) + gather_start("lm", kt_ref, ksems)
    finish(copies)


def step_kernel(
    sl_ref, sk_ref, sq_ref, dl_ref, dk_ref, ld_ref, kd_ref, win_ref,
    rl_ref, rk_ref, own_ref, ql_ref, qk_ref, scal_ref,
    lslots, kslots, kf_slots, lm_slots, lsems, ksems, lgs, kgs, kfs, lms,
):
    greet()
    kf_place = lax.axis_index("kf")
    lm_place = lax.axis_index("lm")
    copies = scatter_start("kf", sl_ref, lslots, lsems)
    copies += scatter_start("lm", sk_ref, kslots, ksems)
    dir_land, dir_key = dl_ref[...], dk_ref[...]
    damped_land = ld_ref[...] * dir_land
    damped_key = kd_ref[...] * dir_key + win_ref[...]
    norm = inner(dir_land, dir_land, dir_key, dir_key)
    energy = sq_ref[0:1, 0:1] + inner(dir_land, damped_land, dir_key, damped_key)
    tile = three_rows(norm, energy, energy)
    tile = sum_all(tile, kf_slots, lm_slots, kfs, lms)
    norm, energy = tile[0:1, 0:1], tile[1:2, 0:1]
    step = norm / energy
    scal_ref[...] = three_rows(norm, energy, step)
    finish(copies)
    prod_land = scatter_total("kf", sl_ref, lslots) + damped_land
    prod_key = scatter_total("lm", sk_ref, kslots) + damped_key
    res_key = dir_key - step * prod_key
    rl_ref[kf_place] = dir_land - step * prod_land
    rk_ref[lm_place] = res_key
    copies = gather_start("kf", rl_ref, lgs) + gather_start("lm", rk_ref, kgs)
    ql_ref[...] = prod_land
    qk_ref[...] = prod_key
    own_ref[...] = res_key
    finish(copies)


def last_kernel(
    sq_ref, dl_ref, dk_ref, ql_ref, qk_ref, ld_ref, kd_ref, win_ref, scal_ref,
    ol_ref, ok_ref, kf_slots, lm_slots, kfs, lms,
):
    greet()
    norm = scal_ref[0:1, 0:1]
    energy = scal_ref[1:2, 0:1]
    step = scal_ref[2:3, 0:1]
    old_land, old_key = dl_ref[...], dk_ref[...]
    prod_land, prod_key = ql_ref[...], qk_ref[...]
    res_land = old_land - step * prod_land
    res_key = old_key - step * prod_key
    own_norm = inner(res_land, res_land, res_key, res_key)
    own_energy = sq_ref[0:1, 0:1] + inner(
        res_land, ld_ref[...] * res_land, res_key, kd_ref[...] * res_key + win_ref[...]
    )
    own_cross = inner(res_land, prod_land, res_key, prod_key)
    tile = three_rows(own_norm, own_energy, own_cross)
    tile = sum_all(tile, kf_slots, lm_slots, kfs, lms)
    norm_next = tile[0:1, 0:1]
    beta = norm_next / norm
    energy_next = tile[1:2, 0:1] + beta * (2.0 * tile[2:3, 0:1] + beta * energy)
    next_step = norm_next / energy_next
    ol_ref[...] = step * old_land + next_step * (res_land + beta * old_land)
    ok_ref[...] = step * old_key + next_step * (res_key + beta * old_key)


def exchange(kernel, identity, outs, scratch, *operands):
    vmem = pl.BlockSpec(memory_space=pltpu.VMEM)
    return pl.pallas_call(
        kernel,
        out_shape=tuple(jax.ShapeDtypeStruct(shape, F32) for shape in outs),
        in_specs=[vmem] * len(operands),
        out_specs=(vmem,) * len(outs),
        scratch_shapes=scratch,
        compiler_params=pltpu.CompilerParams(
            collective_id=identity, has_side_effects=True, vmem_limit_bytes=16 * 2**20
        ),
    )(*operands)


def shards(
    land_rhs, key_rhs, land_damp, key_damp, land_jac, key_jac,
    obs_landmark, obs_keyframe, live_blocks, preint,
):
    state_dev = key_rhs.shape[1]
    kf_count = lax.axis_size("kf")
    lm_count = lax.axis_size("lm")
    key_pos = obs_keyframe // state_dev // kf_count * state_dev + obs_keyframe % state_dev
    key_pos = key_pos[None]
    land_pos = obs_landmark[None]
    land_shape = land_rhs.shape
    dir_land = land_rhs.reshape(-1, LOW)
    damp_land = land_damp.reshape(-1, LOW)
    dir_key = fold_key(key_rhs)
    damp_key = fold_key(key_damp)
    own_land, own_key = dir_land.shape, dir_key.shape
    all_land, all_key = (kf_count,) + own_land, (lm_count,) + own_key

    kf_sems = pltpu.SemaphoreType.DMA((2, kf_count - 1))
    lm_sems = pltpu.SemaphoreType.DMA((2, lm_count - 1))
    slots = [
        pltpu.VMEM((kf_count - 1,) + own_land, F32),
        pltpu.VMEM((lm_count - 1,) + own_key, F32),
    ]
    tiles = [pltpu.VMEM((kf_count, 8, 128), F32), pltpu.VMEM((lm_count, 8, 128), F32)]
    sems = [kf_sems, lm_sems]

    def seen(spread, land_table, key_table):
        return observe(
            spread,
            live_blocks,
            land_table.reshape(-1, LOW),
            key_table.reshape(-1, LOW),
            land_jac,
            key_jac,
            land_pos,
            key_pos,
        )

    land_table, key_table = exchange(
        gather_kernel, 1, (all_land, all_key), sems, dir_land, dir_key
    )
    window = window_product(preint, dir_key)
    sum_land, sum_key, squares = seen(True, land_table, key_table)
    res_land, res_key, own_res, prod_land, prod_key, scal = exchange(
        step_kernel,
        2,
        (all_land, all_key, own_key, own_land, own_key, (8, 128)),
        slots + tiles + sems * 3,
        sum_land.reshape(all_land),
        sum_key.reshape(all_key),
        squares,
        dir_land,
        dir_key,
        damp_land,
        damp_key,
        window,
    )
    window = window_product(preint, own_res)
    (squares,) = seen(False, res_land, res_key)
    sol_land, sol_key = exchange(
        last_kernel,
        3,
        (own_land, own_key),
        tiles + sems,
        squares,
        dir_land,
        dir_key,
        prod_land,
        prod_key,
        damp_land,
        damp_key,
        window,
        scal,
    )
    return sol_land.reshape(land_shape), unfold_key(sol_key)


def solution(mesh):
    split = P(None, ("lm", "kf"))
    line = P(("lm", "kf"))
    in_specs = (split,) * 6 + (line, line, line, split)
    return jax.shard_map(
        shards, mesh=mesh, in_specs=in_specs, out_specs=(split, split), check_vma=False
    )
```
